32 devices in a mesh: req: 8 (over y, x, core), tp: 4 (over z).
Axes of the slice: x: 2, y: 2, z: 4, core: 2. Of those that a mesh axis runs over, the one named last changes fastest.
Arguments:
- tokens: bfloat16 [2048, 2560], P('req'), may hold values from -6 to 6
- norm_gain: float32 [2560], replicated, may hold values from 0.1 to 1.9
- w_query: bfloat16 [2560, 2560], P(None, 'tp')
- w_key: bfloat16 [2560, 640], P(None, 'tp')
- w_value: bfloat16 [2560, 640], P(None, 'tp'), may hold values from -0.125 to 0.125
- page_counts: int32 [4], replicated, may hold values from 1 to 64, 128 in all
- pad_counts: int32 [4], replicated, may hold values from 0 to 15
- page_table: int32 [8, 16], P('req'), may hold values from 0 to 15, each once within a row
Outputs:
- context: bfloat16 [2048, 2560], P('req', 'tp')
- cache: bfloat16 [128, 8, 2560], P(('req', 'tp'))
The draws below stay inside these ranges and needn't reach their ends.
Inputs may be any that keep to these rules, and one draw needn't show every extreme that they name: `page_counts`: each prompt has at least one live slot; the slots of all prompts fill the stream exactly. `page_table`: each row is a permutation; cache slot s of a block belongs to tp index s // 4.
All inputs are finite; a program needn't handle non-finite values.
Results may differ from the reference program's by a relative error of at most 0.012.
Values may be sent and summed in bfloat16 or wider, within the bound.
A program may use at most 64 MiB of HBM per device.

```python
import math
import jax
import jax.numpy as jnp
import numpy as np
from jax import lax

D = 2560
HQ = 32
N_KVH = 8
HD = 80
WINDOW = 4096
PAGE = 16
TOK_DEV = 256
TOKENS = 2048
PPD = 16
NSEQ = 4
LONGEST = 1024
DEPTH = 4
N_REQ = 8


def key_weights(key):
    sub_key = jax.random.fold_in(key, 7177)
    values = jax.random.normal(sub_key, (D, N_KVH * HD), jnp.float32)
    return values * D ** (-0.5)


def draw_w_key(key, part):
    return key_weights(key).astype(jnp.bfloat16)


def draw_w_query(key, part):
    sub_key = jax.random.fold_in(key, 5113)
    spread = 2.4 * D ** (-0.5)
    values = jax.random.normal(sub_key, (D, HQ * HD), jnp.float32) * spread
    return values.astype(jnp.bfloat16)


def touch_ends(values, stream_key, least, top_value):
    index_at = [jax.random.randint(jax.random.fold_in(stream_key, axis), (), 0, length) for axis, length in enumerate(values.shape)]
    widest = values.shape.index(max(values.shape))
    neighbour = index_at[:widest] + [(index_at[widest] + 1) % values.shape[widest]] + index_at[widest + 1:]
    return values.at[tuple(index_at)].set(least).at[tuple(neighbour)].set(top_value)


def levels(own_key, dims, shards, low, top_value):
    def one(axis_at, blocks):
        draws = jax.random.uniform(jax.random.fold_in(jax.random.fold_in(own_key, 6), axis_at), (blocks,), jnp.float32, low / len(shards), top_value / len(shards))
        return jnp.repeat(jnp.exp(draws), dims[axis_at] // blocks).reshape((-1,) + (1,) * (len(dims) - axis_at - 1))

    level = one(*shards[0])
    for cut in shards[1:]:
        level = level * one(*cut)
    return level


def length_profile(count, total, limit, skew):
    weights = [(1 << 20) // math.isqrt(rank ** skew) + 1 for rank in range(2, count + 1)]
    surplus, given = total - limit - (count - 1), [1] * (count - 1)
    while surplus > 0:
        movable = [i for i in range(count - 1) if given[i] < limit]
        pool, budget = sum([weights[i] for i in movable]), surplus
        for i in movable:
            more = min(limit - given[i], max(1, budget * weights[i] // pool), surplus)
            given[i] = given[i] + more
            surplus = surplus - more
    return np.array([limit] + given)


def uneven(key, number_of, total, most, skew):
    if number_of == 2:
        one = jax.random.randint(key, (), max(1, total - most), min(most, total - 1) + 1)
        return jnp.stack([one, total - one])
    sizes = jnp.asarray(length_profile(number_of, total, most, skew), jnp.int32)
    pairs = (number_of - 1) // 2
    donor, taker = sizes[1:1 + 2 * pairs:2], sizes[2:2 + 2 * pairs:2]
    room = jnp.minimum(donor - 1, most - taker)
    moved = jax.random.randint(jax.random.fold_in(key, 1), (pairs,), 0, 1 << 20) % (room + 1)
    sizes = sizes.at[1:1 + 2 * pairs:2].set(donor - moved).at[2:2 + 2 * pairs:2].set(taker + moved)
    return sizes[jax.random.permutation(jax.random.fold_in(key, 2), number_of)]


def scatter_about(rng, shape, scale, bound, shards=(), held_as=jnp.bfloat16):
    array = scale * jax.random.normal(rng, shape, jnp.float32)
    if shards:
        array = array * levels(rng, shape, shards, -0.22, 0.18)
    return jnp.clip(array, -bound, bound).astype(held_as)


def setup_inputs(seed: int = 0) -> dict:
    key_list = jax.random.split(jax.random.key(seed), 9)
    tokens = scatter_about(key_list[0], (TOKENS, D), 1.0, 6.0, ((0, 8),))
    norm_gain = jnp.clip(1.0 + 0.18 * jax.random.normal(key_list[1], (D,), jnp.float32), 0.1, 1.9)
    w_query = draw_w_query(jax.random.fold_in(key_list[8], 71), 0)
    w_key = draw_w_key(jax.random.fold_in(key_list[8], 71), 0)
    w_value = scatter_about(key_list[4], (D, N_KVH * HD), D ** -0.5, 0.125, ((1, 4),))
    page_counts = uneven(key_list[5], NSEQ, TOKENS // PAGE, LONGEST // PAGE, 2).astype(jnp.int32)
    pad_counts = touch_ends(jax.random.randint(key_list[6], (NSEQ,), 0, PAGE), jax.random.fold_in(key_list[6], 1), 0, PAGE - 1).astype(jnp.int32)
    page_table = jax.vmap(lambda own: jax.random.permutation(own, PPD))(jax.random.split(key_list[7], N_REQ)).reshape((N_REQ, PPD)).astype(jnp.int32)
    return {"tokens": tokens, "norm_gain": norm_gain, "w_query": w_query, "w_key": w_key, "w_value": w_value, "page_counts": page_counts, "pad_counts": pad_counts, "page_table": page_table}


NORM_EPS = 1e-05
ROPE_BASE = 10000.0
MASKED_SCORE = -1e+30

def token_meta(slot_index, page_counts, pad_counts):
    prompt_count = page_counts.shape[0]
    slot_counts = page_counts * PAGE
    slot_ends = jnp.cumsum(slot_counts).astype(jnp.int32)
    segment_id = lax.optimization_barrier(jnp.sum((slot_index[:, None] >= slot_ends[None, :]).astype(jnp.int32), axis=1))
    one_hot = (segment_id[:, None] == jnp.arange(prompt_count, dtype=jnp.int32)[None, :]).astype(jnp.int32)
    first_slot = lax.optimization_barrier(jnp.sum(one_hot * (slot_ends - slot_counts)[None, :], axis=1))
    live_count = lax.optimization_barrier(jnp.sum(one_hot * (slot_counts - pad_counts)[None, :], axis=1))
    position = slot_index - first_slot
    inside = slot_index >= 0
    is_live = (position < live_count) & inside
    segment_id = jnp.where(inside, segment_id, -1)
    return (segment_id, position, is_live)

def rotate(vectors, position):
    half_width = vectors.shape[-1] // 2
    frequency = ROPE_BASE ** (-2.0 * jnp.arange(half_width, dtype=jnp.float32) / vectors.shape[-1])
    angles = position.astype(jnp.float32)[:, None, None] * frequency[None, None, :]
    cosine = jnp.cos(angles)
    sine_part = jnp.sin(angles)
    front_half = vectors[..., :half_width]
    back_half = vectors[..., half_width:]
    return jnp.concatenate([front_half * cosine - back_half * sine_part, back_half * cosine + front_half * sine_part], axis=-1)

def project(tokens, norm_gain, w_query, w_key, w_value, position):
    row_count = tokens.shape[0]
    as_float = tokens.astype(jnp.float32)
    normed = (as_float * lax.rsqrt(lax.optimization_barrier(jnp.mean(as_float * as_float, axis=-1, keepdims=True)) + NORM_EPS) * norm_gain).astype(jnp.bfloat16)
    query_rot = jnp.dot(normed, w_query, preferred_element_type=jnp.float32).reshape(row_count, -1, HD)
    query_rot = rotate(query_rot, position).astype(jnp.bfloat16)
    key_rot = jnp.dot(normed, w_key, preferred_element_type=jnp.float32).reshape(row_count, -1, HD)
    key_rot = rotate(key_rot, position).astype(jnp.bfloat16)
    value_rows = jnp.dot(normed, w_value, preferred_element_type=jnp.float32).reshape(row_count, -1, HD).astype(jnp.bfloat16)
    return (query_rot, key_rot, value_rows)

def reference(tokens, norm_gain, w_query, w_key, w_value, page_counts, pad_counts, page_table):
    slot_index = jnp.arange(TOKENS, dtype=jnp.int32)
    segment_id, position, is_live = token_meta(slot_index, page_counts, pad_counts)
    query_rot, key_rot, value_rows = project(tokens, norm_gain, w_query, w_key, w_value, position)
    group_size = HQ // N_KVH
    reach = DEPTH * TOK_DEV
    span = reach + TOK_DEV
    key_pad = jnp.concatenate([jnp.zeros((reach, N_KVH, HD), jnp.bfloat16), key_rot], axis=0)
    value_pad = jnp.concatenate([jnp.zeros((reach, N_KVH, HD), jnp.bfloat16), value_rows], axis=0)
    key_index = jnp.arange(TOKENS + reach, dtype=jnp.int32) - reach
    key_segment, unused_position, key_live = token_meta(key_index, page_counts, pad_counts)
    score_scale = HD ** (-0.5)

    def one_block(block_id):
        first = (block_id * TOK_DEV).astype(jnp.int32)
        queries = lax.dynamic_slice_in_dim(query_rot, first, TOK_DEV, 0).astype(jnp.float32).reshape(TOK_DEV, N_KVH, group_size, HD)
        keys_here = lax.dynamic_slice_in_dim(key_pad, first, span, 0).astype(jnp.float32)
        values_here = lax.dynamic_slice_in_dim(value_pad, first, span, 0).astype(jnp.float32)
        query_index = lax.dynamic_slice_in_dim(slot_index, first, TOK_DEV, 0)
        query_segment = lax.dynamic_slice_in_dim(segment_id, first, TOK_DEV, 0)
        query_live = lax.dynamic_slice_in_dim(is_live, first, TOK_DEV, 0)
        near_index = lax.dynamic_slice_in_dim(key_index, first, span, 0)
        near_segment = lax.dynamic_slice_in_dim(key_segment, first, span, 0)
        near_live = lax.dynamic_slice_in_dim(key_live, first, span, 0)
        allowed = (near_segment[None, :] == query_segment[:, None]) & near_live[None, :]
        allowed = allowed & (near_index[None, :] <= query_index[:, None]) & (query_index[:, None] - near_index[None, :] < WINDOW)

        def one_head(head_id):
            head_queries = lax.dynamic_index_in_dim(queries, head_id, 1, keepdims=False)
            head_keys = lax.dynamic_index_in_dim(keys_here, head_id, 1, keepdims=False)
            head_values = lax.dynamic_index_in_dim(values_here, head_id, 1, keepdims=False)
            scores = jnp.einsum('qjd,kd->jqk', head_queries, head_keys) * score_scale
            scores = jnp.where(allowed[None], scores, MASKED_SCORE)
            row_max = lax.optimization_barrier(jnp.max(scores, axis=-1, keepdims=True))
            probs = jnp.where(allowed[None], jnp.exp(scores - row_max), 0.0)
            prob_total = lax.optimization_barrier(jnp.sum(probs, axis=-1))
            weights = lax.optimization_barrier(probs.astype(jnp.bfloat16)).astype(jnp.float32)
            weighted = jnp.einsum('jqk,kd->jqd', weights, head_values)
            return weighted / prob_total[..., None]
        per_head = lax.map(one_head, jnp.arange(N_KVH, dtype=jnp.int32))
        result = jnp.transpose(per_head, (2, 0, 1, 3)).reshape(TOK_DEV, HQ * HD)
        result = jnp.where(query_live[:, None], result, 0.0)
        return result.astype(jnp.bfloat16)
    blocks = lax.map(one_block, jnp.arange(TOKENS // TOK_DEV, dtype=jnp.int32))
    context = blocks.reshape(TOKENS, HQ * HD)
    packed = jnp.concatenate([key_rot, value_rows], axis=-1)
    live_rows = jnp.where(is_live[:, None, None], packed, jnp.zeros((), jnp.bfloat16))
    page_rows = live_rows.reshape(TOKENS // PAGE, PAGE, N_KVH, 2 * HD).transpose(0, 2, 1, 3).reshape(TOKENS // PAGE, N_KVH, PAGE * 2 * HD)
    target = (jnp.arange(N_REQ, dtype=jnp.int32)[:, None] * PPD + page_table).reshape(-1)
    cache = jnp.zeros_like(page_rows).at[target].set(page_rows)
    return (context, cache)
```

```python
import functools
import math

import jax
import jax.numpy as jnp
from jax import lax
from jax.experimental import pallas as pl
from jax.experimental.pallas import tpu as pltpu
from jax.sharding import PartitionSpec as P

HD = 80
WINDOW = 4096
PAGE = 16
NORM_EPS = 1e-05
ROPE_BASE = 10000.0
MASKED = -1e30
ROW = 2 * HD
ONES = 16
MESH = pl.DeviceIdType.MESH
F32 = jnp.float32
BF16 = jnp.bfloat16


def meta(slot, counts, pads):
    first = jnp.zeros_like(slot)
    last = jnp.zeros_like(slot)
    start = jnp.int32(0)
    for i in range(counts.shape[0]):
        slots = counts[i] * PAGE
        inside = (slot >= start) & (slot < start + slots)
        first = jnp.where(inside, start, first)
        last = jnp.where(inside, start + slots - pads[i] - 1, last)
        start = start + slots
    return first, last


def rotary(u, cosine, sine):
    half = HD // 2
    u1, u2 = u[:half], u[half:]
    return jnp.concatenate([u1 * cosine - u2 * sine, u2 * cosine + u1 * sine], axis=0)


def kernel(
    n_req, n_tp, reach, phases,
    counts, pads, table, gain, tokens_hbm, wk_hbm, wv_hbm, wq_hbm,
    context_ref, cache_ref,
    tokens, wk, wv, wq, kv_own, kv_in, page_out, page_in,
    load_sem, kv_send, kv_recv, page_send, page_recv,
):
    rows = tokens.shape[0]
    kvh = wk.shape[1] // HD
    heads = wq.shape[1] // HD
    group = heads // kvh
    me = lax.axis_index("req")
    my_tp = lax.axis_index("tp")

    loads = [
        pltpu.make_async_copy(src, dst, load_sem.at[i])
        for i, (src, dst) in enumerate(
            ((tokens_hbm, tokens), (wk_hbm, wk), (wv_hbm, wv), (wq_hbm, wq))
        )
    ]
    for load in loads:
        load.start()

    barrier = pltpu.get_barrier_semaphore()
    for d in range(1, reach + 1):
        @pl.when(me + d < n_req)
        def _():
            pl.semaphore_signal(barrier, inc=1, device_id={"req": me + d}, device_id_type=MESH)

        @pl.when(me - d >= 0)
        def _():
            pl.semaphore_signal(barrier, inc=1, device_id={"req": me - d}, device_id_type=MESH)
    for o in range(1, n_tp):
        pl.semaphore_signal(
            barrier, inc=1, device_id={"tp": lax.rem(my_tp + o, n_tp)}, device_id_type=MESH
        )

    block_start = me * rows
    slot = block_start + lax.broadcasted_iota(jnp.int32, (1, rows), 1)
    first, last = meta(slot, counts, pads)
    position = (slot - first).astype(F32)
    live = slot <= last
    high = jnp.minimum(slot, last)
    index = lax.broadcasted_iota(jnp.int32, (HD // 2, 1), 0).astype(F32)
    frequency = jnp.exp(index * (-2.0 * math.log(ROPE_BASE) / HD))
    angle = frequency * position
    cosine, sine = jnp.cos(angle), jnp.sin(angle)

    loads[0].wait()
    x = tokens[...].astype(F32)
    scale = lax.rsqrt(jnp.mean(x * x, axis=-1, keepdims=True) + NORM_EPS)
    tokens[...] = (x * scale * gain[...]).astype(BF16)

    loads[1].wait()
    key = jnp.dot(tokens[...], wk[...], preferred_element_type=F32).T
    loads[2].wait()
    value = jnp.dot(tokens[...], wv[...], preferred_element_type=F32).T
    for g in range(kvh):
        at = g * HD
        kv_own[g * ROW : g * ROW + HD] = rotary(key[at : at + HD], cosine, sine).astype(BF16)
        kv_own[g * ROW + HD : (g + 1) * ROW] = value[at : at + HD].astype(BF16)

    ahead = jnp.minimum(reach, n_req - 1 - me)
    behind = jnp.minimum(reach, me)
    pl.semaphore_wait(barrier, ahead + behind + n_tp - 1)

    def kv_copy(d):
        return pltpu.make_async_remote_copy(
            src_ref=kv_own,
            dst_ref=kv_in.at[d - 1],
            send_sem=kv_send.at[d - 1],
            recv_sem=kv_recv.at[d - 1],
            device_id={"req": me + d},
            device_id_type=MESH,
        )

    for d in range(1, reach + 1):
        @pl.when(me + d < n_req)
        def _():
            kv_copy(d).start()

        @pl.when(me - d < 0)
        def _():
            kv_in[d - 1] = jnp.zeros(kv_in.shape[1:], BF16)

    slots_here = rows // PAGE // n_tp
    live_rows = slots_here * kvh
    fold = 16 // live_rows
    pieces = PAGE // fold
    span = pieces * ROW
    bits = [int(math.log2(v)) for v in (kvh, slots_here, fold, n_tp)]
    r = lax.broadcasted_iota(jnp.int32, (pieces * n_tp * 16, 1), 0)
    h_r = r & (kvh - 1)
    r = r >> bits[0]
    slot_r = r & (slots_here - 1)
    r = r >> bits[1]
    fold_r = r & (fold - 1)
    r = r >> bits[2]
    tp_r = r & (n_tp - 1)
    piece_r = r >> bits[3]
    place_r = h_r + kvh * (fold_r * pieces + piece_r + PAGE * (tp_r * slots_here + slot_r))
    in_block = lax.broadcasted_iota(jnp.int32, (1, rows), 1)
    page_at = jnp.zeros_like(in_block)
    for p in range(rows // PAGE):
        page_at = jnp.where((in_block >> 4) == p, table[0, p], page_at)
    place_t = jnp.where(live, kvh * ((in_block & (PAGE - 1)) + PAGE * page_at), -kvh)
    place_c = jnp.concatenate([place_t + h for h in range(kvh)], axis=1)
    pick = jnp.where(place_r == place_c, 1.0, 0.0).astype(BF16)
    kv_wide = jnp.concatenate([kv_own[g * ROW : (g + 1) * ROW] for g in range(kvh)], axis=1)
    placed = lax.dot_general(
        pick, kv_wide, (((1,), (1,)), ((), ())), preferred_element_type=F32
    )
    wide = jnp.concatenate(
        [placed[i * n_tp * 16 : (i + 1) * n_tp * 16] for i in range(pieces)], axis=1
    ).astype(BF16)
    for t in range(n_tp):
        page_out[t] = wide[t * 16 : (t + 1) * 16]

    def page_copy(o):
        to = lax.rem(my_tp + o, n_tp)
        return pltpu.make_async_remote_copy(
            src_ref=page_out.at[to],
            dst_ref=page_in.at[o],
            send_sem=page_send.at[o],
            recv_sem=page_recv.at[o],
            device_id={"tp": to},
            device_id_type=MESH,
        )

    for o in range(1, n_tp):
        page_copy(o).start()
    page_in[0] = page_out[my_tp]

    loads[3].wait()
    query = jnp.dot(tokens[...], wq[...], preferred_element_type=F32).T
    queries = []
    for g in range(kvh):
        parts = []
        for h in range(g * group, (g + 1) * group):
            parts.append(rotary(query[h * HD : (h + 1) * HD], cosine, sine).astype(BF16))
        queries.append(jnp.concatenate(parts, axis=1))

    factor = math.log2(math.e) / math.sqrt(HD)
    ones = jnp.ones((ONES, rows), BF16)
    state = [None] * kvh
    for blocks in phases:
        bias = []
        for d in blocks:
            if d:
                @pl.when(me - d >= 0)
                def _():
                    kv_copy(d).wait_recv()
            at = slot[:, :1] - d * rows + lax.broadcasted_iota(jnp.int32, (rows, 1), 0)
            ok = (at >= first) & (at <= high)
            if (d + 1) * rows > WINDOW:
                ok = ok & (slot - at < WINDOW)
            bias.append(jnp.where(ok, 0.0, MASKED))
        for g in range(kvh):
            scores, values = [], []
            for d, b in zip(blocks, bias):
                src = kv_own if d == 0 else kv_in.at[d - 1]
                s = lax.dot_general(
                    src[g * ROW : g * ROW + HD], queries[g], (((0,), (0,)), ((), ())),
                    preferred_element_type=F32,
                )
                scores.append(s * factor + jnp.concatenate([b] * group, axis=1))
                values.append(
                    jnp.concatenate([src[g * ROW + HD : (g + 1) * ROW], ones], axis=0)
                )
            top = functools.reduce(
                jnp.maximum, [jnp.max(s, axis=0, keepdims=True) for s in scores]
            )
            if state[g] is not None:
                top = jnp.maximum(top, state[g][0])
            total = None
            for s, v in zip(scores, values):
                w = jnp.exp2(s - top).astype(BF16)
                part = jnp.dot(v, w, preferred_element_type=F32)
                total = part if total is None else total + part
            if state[g] is not None:
                total = total + state[g][1] * jnp.exp2(state[g][0] - top)
            state[g] = (top, total)

    columns = []
    for g in range(kvh):
        acc = state[g][1]
        out = acc[:HD] / acc[HD : HD + 1]
        for j in range(group):
            columns.append(jnp.where(live, out[:, j * rows : (j + 1) * rows], 0.0))
    context_ref[...] = jnp.concatenate(columns, axis=0).T.astype(BF16)

    for o in range(1, n_tp):
        page_copy(o).wait_recv()
    source = lax.broadcasted_iota(jnp.int32, (1, n_tp * 16), 1)
    from_tp = (my_tp - (source >> 4) + n_tp) & (n_tp - 1)
    in_tile = source & 15
    fold_s = in_tile >> (bits[0] + bits[1])
    slot_s = (in_tile >> bits[0]) & (slots_here - 1)
    h_s = in_tile & (kvh - 1)
    goal_s = (slot_s * n_tp + from_tp) * kvh + h_s
    goal = lax.broadcasted_iota(jnp.int32, (slots_here * n_tp * kvh, 1), 0)
    arrived = page_in[...].reshape(n_tp * 16, span)
    lanes = []
    for f in range(fold):
        pick_f = jnp.where((goal == goal_s) & (fold_s == f), 1.0, 0.0).astype(BF16)
        lanes.append(jnp.dot(pick_f, arrived, preferred_element_type=F32))
    pages = jnp.concatenate(lanes, axis=1)
    all_heads = n_tp * kvh
    for s in range(slots_here):
        cache_ref[s] = pages[s * all_heads : (s + 1) * all_heads].astype(BF16)

    for d in range(1, reach + 1):
        @pl.when(me + d < n_req)
        def _():
            kv_copy(d).wait_send()
    for o in range(1, n_tp):
        page_copy(o).wait_send()


def per_device(tokens, norm_gain, w_query, w_key, w_value, page_counts, pad_counts, page_table):
    rows, width = tokens.shape
    n_req, n_tp = lax.axis_size("req"), lax.axis_size("tp")
    longest = min(8 * rows, rows * n_req // 2)
    reach = min(WINDOW, longest) // rows
    phases = [[0], list(range(1, reach + 1))]
    kv_rows = 2 * w_key.shape[1]
    kvh = w_key.shape[1] // HD
    slots_here = rows // PAGE // n_tp
    span = slots_here * kvh * PAGE * ROW // 16
    vmem = pl.BlockSpec(memory_space=pltpu.VMEM)
    smem = pl.BlockSpec(memory_space=pltpu.SMEM)
    hbm = pl.BlockSpec(memory_space=pltpu.HBM)
    return pl.pallas_call(
        functools.partial(kernel, n_req, n_tp, reach, phases),
        out_shape=(
            jax.ShapeDtypeStruct((rows, w_query.shape[1]), BF16),
            jax.ShapeDtypeStruct((slots_here, n_tp * kvh, PAGE * ROW), BF16),
        ),
        in_specs=[smem, smem, smem, vmem, hbm, hbm, hbm, hbm],
        out_specs=(vmem, vmem),
        scratch_shapes=[
            pltpu.VMEM((rows, width), BF16),
            pltpu.VMEM(w_key.shape, BF16),
            pltpu.VMEM(w_value.shape, BF16),
            pltpu.VMEM(w_query.shape, BF16),
            pltpu.VMEM((kv_rows, rows), BF16),
            pltpu.VMEM((reach, kv_rows, rows), BF16),
            pltpu.VMEM((n_tp, 16, span), BF16),
            pltpu.VMEM((n_tp, 16, span), BF16),
            pltpu.SemaphoreType.DMA((4,)),
            pltpu.SemaphoreType.DMA((reach,)),
            pltpu.SemaphoreType.DMA((reach,)),
            pltpu.SemaphoreType.DMA((n_tp,)),
            pltpu.SemaphoreType.DMA((n_tp,)),
        ],
        compiler_params=pltpu.CompilerParams(
            collective_id=0, has_side_effects=True, vmem_limit_bytes=56 * 1024 * 1024
        ),
    )(
        page_counts, pad_counts, page_table, norm_gain.reshape(1, width),
        tokens, w_key, w_value, w_query,
    )


def solution(mesh):
    in_specs = (
        P("req", None),
        P(),
        P(None, "tp"),
        P(None, "tp"),
        P(None, "tp"),
        P(),
        P(),
        P("req", None),
    )
    out_specs = (P("req", "tp"), P(("req", "tp"), None, None))
    return jax.shard_map(
        per_device, mesh=mesh, in_specs=in_specs, out_specs=out_specs, check_vma=False
    )
```

```python
import functools
import math

import jax
import jax.numpy as jnp
from jax import lax
from jax.experimental import pallas as pl
from jax.experimental.pallas import tpu as pltpu
from jax.sharding import PartitionSpec as P

HD = 80
WINDOW = 4096
PAGE = 16
NORM_EPS = 1e-05
ROPE_BASE = 10000.0
MASKED = -1e30
ROW = 2 * HD
ONES = 16
MESH = pl.DeviceIdType.MESH
F32 = jnp.float32
BF16 = jnp.bfloat16


def meta(slot, counts, pads):
    first = jnp.zeros_like(slot)
    last = jnp.zeros_like(slot)
    start = jnp.int32(0)
    for i in range(counts.shape[0]):
        slots = counts[i] * PAGE
        inside = (slot >= start) & (slot < start + slots)
        first = jnp.where(inside, start, first)
        last = jnp.where(inside, start + slots - pads[i] - 1, last)
        start = start + slots
    return first, last


def rotary(u, cosine, sine):
    half = HD // 2
    u1, u2 = u[:half], u[half:]
    return jnp.concatenate([u1 * cosine - u2 * sine, u2 * cosine + u1 * sine], axis=0)


def kernel(
    n_req, n_tp, reach,
    counts, pads, table, gain, tokens_hbm, wk_hbm, wv_hbm, wq_hbm,
    context_ref, pages_ref,
    tokens, wkv, wq, kv_own, kv_in, page_out, page_in,
    load_sem, kv_send, kv_recv, hand_send, page_send, page_recv,
):
    rows = tokens.shape[0]
    kvh = wkv.shape[0] // ROW
    heads = wq.shape[1] // HD
    group = heads // kvh
    me = lax.axis_index("req")
    my_tp = lax.axis_index("tp")

    odd = lax.rem(me, 2)
    partner = me + 1 - 2 * odd
    evens = range(2, reach + 1, 2)

    kv_width = kvh * HD
    loads = [
        pltpu.make_async_copy(src, dst, load_sem.at[i])
        for i, (src, dst) in enumerate(
            (
                (tokens_hbm, tokens),
                (wk_hbm, wkv.at[:kv_width]),
                (wv_hbm, wkv.at[kv_width:]),
                (wq_hbm, wq),
            )
        )
    ]
    for load in loads:
        load.start()

    barrier = pltpu.get_barrier_semaphore()
    pl.semaphore_signal(barrier, inc=1, device_id={"req": partner}, device_id_type=MESH)
    for d in evens:
        @pl.when(me + d < n_req)
        def _():
            pl.semaphore_signal(barrier, inc=1, device_id={"req": me + d}, device_id_type=MESH)

        @pl.when(me - d >= 0)
        def _():
            pl.semaphore_signal(barrier, inc=1, device_id={"req": me - d}, device_id_type=MESH)
    for o in range(1, n_tp):
        pl.semaphore_signal(
            barrier, inc=1, device_id={"tp": lax.rem(my_tp + o, n_tp)}, device_id_type=MESH
        )

    block_start = me * rows
    slot = block_start + lax.broadcasted_iota(jnp.int32, (1, rows), 1)
    first, last = meta(slot, counts, pads)
    position = (slot - first).astype(F32)
    live = slot <= last
    high = jnp.minimum(slot, last)
    index = lax.broadcasted_iota(jnp.int32, (HD // 2, 1), 0).astype(F32)
    frequency = jnp.exp(index * (-2.0 * math.log(ROPE_BASE) / HD))
    angle = frequency * position
    cosine, sine = jnp.cos(angle), jnp.sin(angle)

    loads[0].wait()
    x = tokens[...].astype(F32)
    scale = lax.rsqrt(jnp.mean(x * x, axis=-1, keepdims=True) + NORM_EPS)
    tokens[...] = (x * scale * gain[...].reshape(1, -1)).astype(BF16)

    loads[1].wait()
    loads[2].wait()
    both = lax.dot_general(
        wkv[...], tokens[...], (((1,), (1,)), ((), ())), preferred_element_type=F32
    )
    key, value = both[:kv_width], both[kv_width:]
    for g in range(kvh):
        at = g * HD
        kv_own[g * ROW : g * ROW + HD] = rotary(key[at : at + HD], cosine, sine).astype(BF16)
        kv_own[g * ROW + HD : (g + 1) * ROW] = value[at : at + HD].astype(BF16)

    ahead = jnp.minimum(reach, n_req - 1 - me) >> 1
    behind = jnp.minimum(reach, me) >> 1
    pl.semaphore_wait(barrier, ahead + behind + n_tp)

    def head(ref, g):
        return ref.at[g * ROW : (g + 1) * ROW]

    def kv_copy(d, g):
        return pltpu.make_async_remote_copy(
            src_ref=head(kv_own, g),
            dst_ref=kv_in.at[d - 1, g * ROW : (g + 1) * ROW],
            send_sem=kv_send.at[d - 1, g],
            recv_sem=kv_recv.at[d - 1, g],
            device_id={"req": me + d},
            device_id_type=MESH,
        )

    def hand_on(e, g):
        to = e - 2 * odd
        return pltpu.make_async_remote_copy(
            src_ref=kv_in.at[e - 1, g * ROW : (g + 1) * ROW] if e else head(kv_own, g),
            dst_ref=kv_in.at[to, g * ROW : (g + 1) * ROW],
            send_sem=hand_send.at[e, g],
            recv_sem=kv_recv.at[to, g],
            device_id={"req": partner},
            device_id_type=MESH,
        )

    def hands_on(e):
        if e == 0:
            return odd == 0
        if e == reach:
            return (odd == 1) & (me - e >= 0)
        return me - e >= 0

    for g in range(kvh):
        for d in evens:
            @pl.when(me + d < n_req)
            def _():
                kv_copy(d, g).start()

        @pl.when(hands_on(0))
        def _():
            hand_on(0, g).start()

    for d in range(1, reach + 1):
        @pl.when(me - d < 0)
        def _():
            kv_in[d - 1] = jnp.zeros(kv_in.shape[1:], BF16)

    slots_here = rows // PAGE // n_tp
    live_rows = slots_here * kvh
    fold = 16 // live_rows
    pieces = PAGE // fold
    span = pieces * ROW
    bits = [int(math.log2(v)) for v in (kvh, slots_here, fold, n_tp)]
    r = lax.broadcasted_iota(jnp.int32, (pieces * n_tp * 16, 1), 0)
    h_r = r & (kvh - 1)
    r = r >> bits[0]
    slot_r = r & (slots_here - 1)
    r = r >> bits[1]
    fold_r = r & (fold - 1)
    r = r >> bits[2]
    tp_r = r & (n_tp - 1)
    piece_r = r >> bits[3]
    place_r = h_r + kvh * (fold_r * pieces + piece_r + PAGE * (tp_r * slots_here + slot_r))
    in_block = lax.broadcasted_iota(jnp.int32, (1, rows), 1)
    page_at = jnp.zeros_like(in_block)
    for p in range(rows // PAGE):
        page_at = jnp.where((in_block >> 4) == p, table[0, p], page_at)
    place_t = jnp.where(live, kvh * ((in_block & (PAGE - 1)) + PAGE * page_at), -kvh)
    place_c = jnp.concatenate([place_t + h for h in range(kvh)], axis=1)
    pick = jnp.where(place_r == place_c, 1.0, 0.0).astype(BF16)
    kv_wide = jnp.concatenate([kv_own[g * ROW : (g + 1) * ROW] for g in range(kvh)], axis=1)
    placed = lax.dot_general(
        pick, kv_wide, (((1,), (1,)), ((), ())), preferred_element_type=F32
    )
    wide = jnp.concatenate(
        [placed[i * n_tp * 16 : (i + 1) * n_tp * 16] for i in range(pieces)], axis=1
    ).astype(BF16)
    for t in range(n_tp):
        page_out[t] = wide[t * 16 : (t + 1) * 16]

    def page_copy(o):
        to = lax.rem(my_tp + o, n_tp)
        return pltpu.make_async_remote_copy(
            src_ref=page_out.at[to],
            dst_ref=page_in.at[o],
            send_sem=page_send.at[o],
            recv_sem=page_recv.at[o],
            device_id={"tp": to},
            device_id_type=MESH,
        )

    for o in range(1, n_tp):
        page_copy(o).start()
    page_in[0] = page_out[my_tp]

    loads[3].wait()
    query = jnp.dot(tokens[...], wq[...], preferred_element_type=F32).T
    queries = []
    for g in range(kvh):
        parts = []
        for h in range(g * group, (g + 1) * group):
            parts.append(rotary(query[h * HD : (h + 1) * HD], cosine, sine).astype(BF16))
        queries.append(jnp.concatenate(parts, axis=1))

    factor = math.log2(math.e) / math.sqrt(HD)
    ones = jnp.ones((ONES, rows), BF16)
    state = [None] * kvh

    def bias_of(d):
        at = block_start - d * rows + lax.broadcasted_iota(jnp.int32, (rows, 1), 0)
        ok = (at >= first) & (at <= high)
        if (d + 1) * rows > WINDOW:
            ok = ok & (slot - at < WINDOW)
        return jnp.where(ok, 0.0, MASKED)

    def attend(g, blocks, biases):
        scores, values = [], []
        for d, b in zip(blocks, biases):
            src = kv_own if d == 0 else kv_in.at[d - 1]
            s = lax.dot_general(
                src[g * ROW : g * ROW + HD], queries[g], (((0,), (0,)), ((), ())),
                preferred_element_type=F32,
            )
            scores.append(s * factor + jnp.concatenate([b] * group, axis=1))
            values.append(jnp.concatenate([src[g * ROW + HD : (g + 1) * ROW], ones], axis=0))
        top = functools.reduce(
            jnp.maximum, [jnp.max(s, axis=0, keepdims=True) for s in scores]
        )
        if state[g] is not None:
            top = jnp.maximum(top, state[g][0])
        total = None
        for s, v in zip(scores, values):
            w = jnp.exp2(s - top).astype(BF16)
            part = jnp.dot(v, w, preferred_element_type=F32)
            total = part if total is None else total + part
        if state[g] is not None:
            total = total + state[g][1] * jnp.exp2(state[g][0] - top)
        state[g] = (top, total)

    own_bias = [bias_of(0)]
    for g in range(kvh):
        attend(g, [0], own_bias)
        for d in evens:
            @pl.when(me - d >= 0)
            def _():
                kv_copy(d, g).wait_recv()

            @pl.when(hands_on(d))
            def _():
                hand_on(d, g).start()
    biases = [bias_of(d) for d in evens]
    for g in range(kvh):
        attend(g, list(evens), biases)
    odds = range(1, reach + 1, 2)
    biases = [bias_of(d) for d in odds]
    for g in range(kvh):
        for d in odds:
            @pl.when(me - d >= 0)
            def _():
                kv_copy(d, g).wait_recv()
        attend(g, list(odds), biases)
        acc = state[g][1]
        out = acc[:HD] / acc[HD : HD + 1]
        for j in range(group):
            at = (g * group + j) * HD
            context_ref[at : at + HD] = jnp.where(
                live, out[:, j * rows : (j + 1) * rows], 0.0
            ).astype(BF16)

    for o in range(1, n_tp):
        page_copy(o).wait_recv()
    pages_ref[...] = page_in[...]

    for g in range(kvh):
        for d in evens:
            @pl.when(me + d < n_req)
            def _():
                kv_copy(d, g).wait_send()
        for e in range(0, reach + 1, 2):
            @pl.when(hands_on(e))
            def _():
                hand_on(e, g).wait_send()
    for o in range(1, n_tp):
        page_copy(o).wait_send()


def finish(n_tp, kvh, context_t, page_in, context_ref, cache_ref):
    context_ref[...] = context_t[...].T
    slots_here = cache_ref.shape[0]
    fold = 16 // (slots_here * kvh)
    bits = [int(math.log2(v)) for v in (kvh, slots_here)]
    my_tp = lax.axis_index("tp")
    source = lax.broadcasted_iota(jnp.int32, (1, n_tp * 16), 1)
    from_tp = (my_tp - (source >> 4) + n_tp) & (n_tp - 1)
    in_tile = source & 15
    fold_s = in_tile >> (bits[0] + bits[1])
    slot_s = (in_tile >> bits[0]) & (slots_here - 1)
    h_s = in_tile & (kvh - 1)
    goal_s = (slot_s * n_tp + from_tp) * kvh + h_s
    goal = lax.broadcasted_iota(jnp.int32, (slots_here * n_tp * kvh, 1), 0)
    arrived = page_in[...].reshape(n_tp * 16, page_in.shape[2])
    lanes = []
    for f in range(fold):
        pick_f = jnp.where((goal == goal_s) & (fold_s == f), 1.0, 0.0).astype(BF16)
        lanes.append(jnp.dot(pick_f, arrived, preferred_element_type=F32))
    pages = jnp.concatenate(lanes, axis=1)
    all_heads = n_tp * kvh
    for s in range(slots_here):
        cache_ref[s] = pages[s * all_heads : (s + 1) * all_heads].astype(BF16)


def per_device(tokens, norm_gain, w_query, w_key, w_value, page_counts, pad_counts, page_table):
    rows, width = tokens.shape
    n_req, n_tp = lax.axis_size("req"), lax.axis_size("tp")
    longest = min(8 * rows, rows * n_req // 2)
    reach = min(WINDOW, longest) // rows
    assert reach % 2 == 0 and n_req % 2 == 0
    kv_rows = 2 * w_key.shape[1]
    kvh = w_key.shape[1] // HD
    slots_here = rows // PAGE // n_tp
    span = slots_here * kvh * PAGE * ROW // 16
    vmem = pl.BlockSpec(memory_space=pltpu.VMEM)
    smem = pl.BlockSpec(memory_space=pltpu.SMEM)
    hbm = pl.BlockSpec(memory_space=pltpu.HBM)
    context_t, pages = pl.pallas_call(
        functools.partial(kernel, n_req, n_tp, reach),
        out_shape=(
            jax.ShapeDtypeStruct((w_query.shape[1], rows), BF16),
            jax.ShapeDtypeStruct((n_tp, 16, span), BF16),
        ),
        in_specs=[smem, smem, smem, vmem, hbm, hbm, hbm, hbm],
        out_specs=(vmem, vmem),
        scratch_shapes=[
            pltpu.VMEM((rows, width), BF16),
            pltpu.VMEM((kv_rows, width), BF16),
            pltpu.VMEM(w_query.shape, BF16),
            pltpu.VMEM((kv_rows, rows), BF16),
            pltpu.VMEM((reach, kv_rows, rows), BF16),
            pltpu.VMEM((n_tp, 16, span), BF16),
            pltpu.VMEM((n_tp, 16, span), BF16),
            pltpu.SemaphoreType.DMA((4,)),
            pltpu.SemaphoreType.DMA((reach, kvh)),
            pltpu.SemaphoreType.DMA((reach, kvh)),
            pltpu.SemaphoreType.DMA((reach + 1, kvh)),
            pltpu.SemaphoreType.DMA((n_tp,)),
            pltpu.SemaphoreType.DMA((n_tp,)),
        ],
        compiler_params=pltpu.CompilerParams(
            collective_id=0, has_side_effects=True, vmem_limit_bytes=56 * 1024 * 1024
        ),
    )(
        page_counts, pad_counts, page_table, norm_gain,
        tokens, w_key.T, w_value.T, w_query,
    )
    return pl.pallas_call(
        functools.partial(finish, n_tp, kvh),
        out_shape=(
            jax.ShapeDtypeStruct((rows, w_query.shape[1]), BF16),
            jax.ShapeDtypeStruct((slots_here, n_tp * kvh, PAGE * ROW), BF16),
        ),
        in_specs=[vmem, vmem],
        out_specs=(vmem, vmem),
        compiler_params=pltpu.CompilerParams(vmem_limit_bytes=32 * 1024 * 1024),
    )(context_t, pages)


def solution(mesh):
    in_specs = (
        P("req", None),
        P(),
        P(None, "tp"),
        P(None, "tp"),
        P(None, "tp"),
        P(),
        P(),
        P("req", None),
    )
    out_specs = (P("req", "tp"), P(("req", "tp"), None, None))
    return jax.shard_map(
        per_device, mesh=mesh, in_specs=in_specs, out_specs=out_specs, check_vma=False
    )
```

```python
import functools
import math

import jax
import jax.numpy as jnp
from jax import lax
from jax.experimental import pallas as pl
from jax.experimental.pallas import tpu as pltpu
from jax.sharding import PartitionSpec as P

HD = 80
WINDOW = 4096
PAGE = 16
NORM_EPS = 1e-05
ROPE_BASE = 10000.0
MASKED = -1e30
ROW = 2 * HD
ONES = 16
MESH = pl.DeviceIdType.MESH
F32 = jnp.float32
BF16 = jnp.bfloat16


def meta(slot, counts, pads):
    first = jnp.zeros_like(slot)
    last = jnp.zeros_like(slot)
    start = jnp.int32(0)
    for i in range(counts.shape[0]):
        slots = counts[i] * PAGE
        inside = (slot >= start) & (slot < start + slots)
        first = jnp.where(inside, start, first)
        last = jnp.where(inside, start + slots - pads[i] - 1, last)
        start = start + slots
    return first, last


def rotary(u, cosine, sine):
    half = HD // 2
    u1, u2 = u[:half], u[half:]
    return jnp.concatenate([u1 * cosine - u2 * sine, u2 * cosine + u1 * sine], axis=0)


def kernel(
    n_req, n_tp, reach,
    counts, pads, table, gain, tokens_hbm, wk_hbm, wv_hbm, wq_hbm,
    context_ref, pages_ref,
    tokens, wkv, wq, kv_own, kv_in, page_out, page_in,
    load_sem, kv_send, kv_recv, hand_send, back_send, page_send, page_recv,
):
    rows = tokens.shape[0]
    kvh = wkv.shape[0] // ROW
    heads = wq.shape[1] // HD
    group = heads // kvh
    me = lax.axis_index("req")
    my_tp = lax.axis_index("tp")

    odd = lax.rem(me, 2)
    partner = me + 1 - 2 * odd
    evens = range(2, reach + 1, 2)

    kv_width = kvh * HD
    loads = [
        pltpu.make_async_copy(src, dst, load_sem.at[i])
        for i, (src, dst) in enumerate(
            (
                (tokens_hbm, tokens),
                (wk_hbm, wkv.at[:kv_width]),
                (wv_hbm, wkv.at[kv_width:]),
                (wq_hbm, wq),
            )
        )
    ]
    for load in loads:
        load.start()

    barrier = pltpu.get_barrier_semaphore()
    pl.semaphore_signal(barrier, inc=1, device_id={"req": partner}, device_id_type=MESH)
    for d in evens:
        @pl.when(me + d < n_req)
        def _():
            pl.semaphore_signal(barrier, inc=1, device_id={"req": me + d}, device_id_type=MESH)

        @pl.when(me - d >= 0)
        def _():
            pl.semaphore_signal(barrier, inc=1, device_id={"req": me - d}, device_id_type=MESH)
    for o in range(1, n_tp):
        pl.semaphore_signal(
            barrier, inc=1, device_id={"tp": lax.rem(my_tp + o, n_tp)}, device_id_type=MESH
        )

    block_start = me * rows
    slot = block_start + lax.broadcasted_iota(jnp.int32, (1, rows), 1)
    first, last = meta(slot, counts, pads)
    position = (slot - first).astype(F32)
    live = slot <= last
    high = jnp.minimum(slot, last)
    index = lax.broadcasted_iota(jnp.int32, (HD // 2, 1), 0).astype(F32)
    frequency = jnp.exp(index * (-2.0 * math.log(ROPE_BASE) / HD))
    angle = frequency * position
    cosine, sine = jnp.cos(angle), jnp.sin(angle)

    loads[0].wait()
    x = tokens[...].astype(F32)
    scale = lax.rsqrt(jnp.mean(x * x, axis=-1, keepdims=True) + NORM_EPS)
    tokens[...] = (x * scale * gain[...].reshape(1, -1)).astype(BF16)

    loads[1].wait()
    loads[2].wait()
    both = lax.dot_general(
        wkv[...], tokens[...], (((1,), (1,)), ((), ())), preferred_element_type=F32
    )
    key, value = both[:kv_width], both[kv_width:]
    for g in range(kvh):
        at = g * HD
        kv_own[g * ROW : g * ROW + HD] = rotary(key[at : at + HD], cosine, sine).astype(BF16)
        kv_own[g * ROW + HD : (g + 1) * ROW] = value[at : at + HD].astype(BF16)

    ahead = jnp.minimum(reach, n_req - 1 - me) >> 1
    behind = jnp.minimum(reach, me) >> 1
    pl.semaphore_wait(barrier, ahead + behind + n_tp)

    def head(ref, g):
        return ref.at[g * ROW : (g + 1) * ROW]

    def kv_copy(d, g):
        return pltpu.make_async_remote_copy(
            src_ref=head(kv_own, g),
            dst_ref=kv_in.at[d - 1, g * ROW : (g + 1) * ROW],
            send_sem=kv_send.at[d - 1, g],
            recv_sem=kv_recv.at[d - 1, g],
            device_id={"req": me + d},
            device_id_type=MESH,
        )

    def hand_on(e, g):
        to = e - 2 * odd
        return pltpu.make_async_remote_copy(
            src_ref=kv_in.at[e - 1, g * ROW : (g + 1) * ROW] if e else head(kv_own, g),
            dst_ref=kv_in.at[to, g * ROW : (g + 1) * ROW],
            send_sem=hand_send.at[e, g],
            recv_sem=kv_recv.at[to, g],
            device_id={"req": partner},
            device_id_type=MESH,
        )

    def hands_on(e):
        if e == 0:
            return odd == 0
        if e == reach:
            return (odd == 1) & (me - e >= 0)
        return me - e >= 0

    square = n_req == 8 and reach == 4

    def sends(d, g):
        go = me + d < n_req
        if square and d == 2 and g == 0:
            go = go & ((me < 2) | (me > 3))
        return go

    def pass_back(g):
        return pltpu.make_async_remote_copy(
            src_ref=kv_in.at[3, g * ROW : (g + 1) * ROW],
            dst_ref=kv_in.at[1, g * ROW : (g + 1) * ROW],
            send_sem=back_send.at[g],
            recv_sem=kv_recv.at[1, g],
            device_id={"req": me - 2},
            device_id_type=MESH,
        )

    for g in range(kvh):
        for d in evens:
            @pl.when(sends(d, g))
            def _():
                kv_copy(d, g).start()

        @pl.when(hands_on(0))
        def _():
            hand_on(0, g).start()

    for d in range(1, reach + 1):
        @pl.when(me - d < 0)
        def _():
            kv_in[d - 1] = jnp.zeros(kv_in.shape[1:], BF16)

    slots_here = rows // PAGE // n_tp
    live_rows = slots_here * kvh
    fold = 16 // live_rows
    pieces = PAGE // fold
    span = pieces * ROW
    bits = [int(math.log2(v)) for v in (kvh, slots_here, fold, n_tp)]
    r = lax.broadcasted_iota(jnp.int32, (pieces * n_tp * 16, 1), 0)
    h_r = r & (kvh - 1)
    r = r >> bits[0]
    slot_r = r & (slots_here - 1)
    r = r >> bits[1]
    fold_r = r & (fold - 1)
    r = r >> bits[2]
    tp_r = r & (n_tp - 1)
    piece_r = r >> bits[3]
    place_r = h_r + kvh * (fold_r * pieces + piece_r + PAGE * (tp_r * slots_here + slot_r))
    in_block = lax.broadcasted_iota(jnp.int32, (1, rows), 1)
    page_at = jnp.zeros_like(in_block)
    for p in range(rows // PAGE):
        page_at = jnp.where((in_block >> 4) == p, table[0, p], page_at)
    place_t = jnp.where(live, kvh * ((in_block & (PAGE - 1)) + PAGE * page_at), -kvh)
    place_c = jnp.concatenate([place_t + h for h in range(kvh)], axis=1)
    pick = jnp.where(place_r == place_c, 1.0, 0.0).astype(BF16)
    kv_wide = jnp.concatenate([kv_own[g * ROW : (g + 1) * ROW] for g in range(kvh)], axis=1)
    placed = lax.dot_general(
        pick, kv_wide, (((1,), (1,)), ((), ())), preferred_element_type=F32
    )
    wide = jnp.concatenate(
        [placed[i * n_tp * 16 : (i + 1) * n_tp * 16] for i in range(pieces)], axis=1
    ).astype(BF16)
    for t in range(n_tp):
        page_out[t] = wide[t * 16 : (t + 1) * 16]

    def page_copy(o):
        to = lax.rem(my_tp + o, n_tp)
        return pltpu.make_async_remote_copy(
            src_ref=page_out.at[to],
            dst_ref=page_in.at[o],
            send_sem=page_send.at[o],
            recv_sem=page_recv.at[o],
            device_id={"tp": to},
            device_id_type=MESH,
        )

    for o in range(1, n_tp):
        page_copy(o).start()
    page_in[0] = page_out[my_tp]

    loads[3].wait()
    query = jnp.dot(tokens[...], wq[...], preferred_element_type=F32).T
    queries = []
    for g in range(kvh):
        parts = []
        for h in range(g * group, (g + 1) * group):
            parts.append(rotary(query[h * HD : (h + 1) * HD], cosine, sine).astype(BF16))
        queries.append(jnp.concatenate(parts, axis=1))

    factor = math.log2(math.e) / math.sqrt(HD)
    ones = jnp.ones((ONES, rows), BF16)
    state = [None] * kvh

    def bias_of(d):
        at = block_start - d * rows + lax.broadcasted_iota(jnp.int32, (rows, 1), 0)
        ok = (at >= first) & (at <= high)
        if (d + 1) * rows > WINDOW:
            ok = ok & (slot - at < WINDOW)
        return jnp.where(ok, 0.0, MASKED)

    def attend(g, blocks, biases):
        scores, values = [], []
        for d, b in zip(blocks, biases):
            src = kv_own if d == 0 else kv_in.at[d - 1]
            s = lax.dot_general(
                src[g * ROW : g * ROW + HD], queries[g], (((0,), (0,)), ((), ())),
                preferred_element_type=F32,
            )
            scores.append(s * factor + jnp.concatenate([b] * group, axis=1))
            values.append(jnp.concatenate([src[g * ROW + HD : (g + 1) * ROW], ones], axis=0))
        top = functools.reduce(
            jnp.maximum, [jnp.max(s, axis=0, keepdims=True) for s in scores]
        )
        if state[g] is not None:
            top = jnp.maximum(top, state[g][0])
        total = None
        for s, v in zip(scores, values):
            w = jnp.exp2(s - top).astype(BF16)
            part = jnp.dot(v, w, preferred_element_type=F32)
            total = part if total is None else total + part
        if state[g] is not None:
            total = total + state[g][1] * jnp.exp2(state[g][0] - top)
        state[g] = (top, total)

    own_bias = [bias_of(0)]
    if square:
        @pl.when(me > 5)
        def _():
            kv_copy(4, 0).wait_recv()
            pass_back(0).start()
    for g in range(kvh):
        attend(g, [0], own_bias)
    for g in reversed(range(kvh)):
        for d in evens:
            due = me - d >= 0
            if square and d == 4 and g == 0:
                due = due & (me < 6)

            @pl.when(due)
            def _():
                kv_copy(d, g).wait_recv()

            @pl.when(hands_on(d))
            def _():
                hand_on(d, g).start()
    biases = [bias_of(d) for d in evens]
    for g in range(kvh):
        attend(g, list(evens), biases)
    odds = range(1, reach + 1, 2)
    biases = [bias_of(d) for d in odds]
    for g in range(kvh):
        for d in odds:
            @pl.when(me - d >= 0)
            def _():
                kv_copy(d, g).wait_recv()
        attend(g, list(odds), biases)
        acc = state[g][1]
        out = acc[:HD] / acc[HD : HD + 1]
        for j in range(group):
            at = (g * group + j) * HD
            context_ref[at : at + HD] = jnp.where(
                live, out[:, j * rows : (j + 1) * rows], 0.0
            ).astype(BF16)

    for o in range(1, n_tp):
        page_copy(o).wait_recv()
    pages_ref[...] = page_in[...]

    for g in range(kvh):
        for d in evens:
            @pl.when(sends(d, g))
            def _():
                kv_copy(d, g).wait_send()
        for e in range(0, reach + 1, 2):
            @pl.when(hands_on(e))
            def _():
                hand_on(e, g).wait_send()
    if square:
        @pl.when(me > 5)
        def _():
            pass_back(0).wait_send()
    for o in range(1, n_tp):
        page_copy(o).wait_send()


def finish(n_tp, kvh, context_hbm, page_hbm, context_ref, cache_ref, context_t, page_in, load_sem):
    loads = [
        pltpu.make_async_copy(context_hbm, context_t, load_sem.at[0]),
        pltpu.make_async_copy(page_hbm, page_in, load_sem.at[1]),
    ]
    for load in loads:
        load.start()
    loads[0].wait()
    context_ref[...] = context_t[...].T
    slots_here = cache_ref.shape[0]
    fold = 16 // (slots_here * kvh)
    bits = [int(math.log2(v)) for v in (kvh, slots_here)]
    my_tp = lax.axis_index("tp")
    source = lax.broadcasted_iota(jnp.int32, (1, n_tp * 16), 1)
    from_tp = (my_tp - (source >> 4) + n_tp) & (n_tp - 1)
    in_tile = source & 15
    fold_s = in_tile >> (bits[0] + bits[1])
    slot_s = (in_tile >> bits[0]) & (slots_here - 1)
    h_s = in_tile & (kvh - 1)
    goal_s = (slot_s * n_tp + from_tp) * kvh + h_s
    goal = lax.broadcasted_iota(jnp.int32, (slots_here * n_tp * kvh, 1), 0)
    loads[1].wait()
    arrived = page_in[...].reshape(n_tp * 16, page_in.shape[2])
    lanes = []
    for f in range(fold):
        pick_f = jnp.where((goal == goal_s) & (fold_s == f), 1.0, 0.0).astype(BF16)
        lanes.append(jnp.dot(pick_f, arrived, preferred_element_type=F32))
    pages = jnp.concatenate(lanes, axis=1)
    all_heads = n_tp * kvh
    for s in range(slots_here):
        cache_ref[s] = pages[s * all_heads : (s + 1) * all_heads].astype(BF16)


def per_device(tokens, norm_gain, w_query, w_key, w_value, page_counts, pad_counts, page_table):
    rows, width = tokens.shape
    n_req, n_tp = lax.axis_size("req"), lax.axis_size("tp")
    longest = min(8 * rows, rows * n_req // 2)
    reach = min(WINDOW, longest) // rows
    assert reach % 2 == 0 and n_req % 2 == 0
    kv_rows = 2 * w_key.shape[1]
    kvh = w_key.shape[1] // HD
    slots_here = rows // PAGE // n_tp
    span = slots_here * kvh * PAGE * ROW // 16
    vmem = pl.BlockSpec(memory_space=pltpu.VMEM)
    smem = pl.BlockSpec(memory_space=pltpu.SMEM)
    hbm = pl.BlockSpec(memory_space=pltpu.HBM)
    context_t, pages = pl.pallas_call(
        functools.partial(kernel, n_req, n_tp, reach),
        out_shape=(
            jax.ShapeDtypeStruct((w_query.shape[1], rows), BF16),
            jax.ShapeDtypeStruct((n_tp, 16, span), BF16),
        ),
        in_specs=[smem, smem, smem, vmem, hbm, hbm, hbm, hbm],
        out_specs=(vmem, vmem),
        scratch_shapes=[
            pltpu.VMEM((rows, width), BF16),
            pltpu.VMEM((kv_rows, width), BF16),
            pltpu.VMEM(w_query.shape, BF16),
            pltpu.VMEM((kv_rows, rows), BF16),
            pltpu.VMEM((reach, kv_rows, rows), BF16),
            pltpu.VMEM((n_tp, 16, span), BF16),
            pltpu.VMEM((n_tp, 16, span), BF16),
            pltpu.SemaphoreType.DMA((4,)),
            pltpu.SemaphoreType.DMA((reach, kvh)),
            pltpu.SemaphoreType.DMA((reach, kvh)),
            pltpu.SemaphoreType.DMA((reach + 1, kvh)),
            pltpu.SemaphoreType.DMA((kvh,)),
            pltpu.SemaphoreType.DMA((n_tp,)),
            pltpu.SemaphoreType.DMA((n_tp,)),
        ],
        compiler_params=pltpu.CompilerParams(
            collective_id=0, has_side_effects=True, vmem_limit_bytes=56 * 1024 * 1024
        ),
    )(
        page_counts, pad_counts, page_table, norm_gain,
        tokens, w_key.T, w_value.T, w_query,
    )
    return pl.pallas_call(
        functools.partial(finish, n_tp, kvh),
        out_shape=(
            jax.ShapeDtypeStruct((rows, w_query.shape[1]), BF16),
            jax.ShapeDtypeStruct((slots_here, n_tp * kvh, PAGE * ROW), BF16),
        ),
        in_specs=[hbm, hbm],
        out_specs=(vmem, vmem),
        scratch_shapes=[
            pltpu.VMEM((w_query.shape[1], rows), BF16),
            pltpu.VMEM((n_tp, 16, span), BF16),
            pltpu.SemaphoreType.DMA((2,)),
        ],
        compiler_params=pltpu.CompilerParams(vmem_limit_bytes=56 * 1024 * 1024),
    )(context_t, pages)


def solution(mesh):
    in_specs = (
        P("req", None),
        P(),
        P(None, "tp"),
        P(None, "tp"),
        P(None, "tp"),
        P(),
        P(),
        P("req", None),
    )
    out_specs = (P("req", "tp"), P(("req", "tp"), None, None))
    return jax.shard_map(
        per_device, mesh=mesh, in_specs=in_specs, out_specs=out_specs, check_vma=False
    )
```

```python
import functools
import math

import jax
import jax.numpy as jnp
from jax import lax
from jax.experimental import pallas as pl
from jax.experimental.pallas import tpu as pltpu
from jax.sharding import PartitionSpec as P

HD = 80
WINDOW = 4096
PAGE = 16
NORM_EPS = 1e-05
ROPE_BASE = 10000.0
MASKED = -1e30
ROW = 2 * HD
ONES = 16
MESH = pl.DeviceIdType.MESH
F32 = jnp.float32
BF16 = jnp.bfloat16


def meta(slot, counts, pads):
    first = jnp.zeros_like(slot)
    last = jnp.zeros_like(slot)
    start = jnp.int32(0)
    for i in range(counts.shape[0]):
        slots = counts[i] * PAGE
        inside = (slot >= start) & (slot < start + slots)
        first = jnp.where(inside, start, first)
        last = jnp.where(inside, start + slots - pads[i] - 1, last)
        start = start + slots
    return first, last


def rotary(u, cosine, sine):
    half = HD // 2
    u1, u2 = u[:half], u[half:]
    return jnp.concatenate([u1 * cosine - u2 * sine, u2 * cosine + u1 * sine], axis=0)


def kernel(
    n_req, n_tp, reach,
    counts, pads, table, gain, tokens_hbm, wk_hbm, wv_hbm, wq_hbm,
    context_ref, pages_ref,
    tokens, wkv, wq, kv_own, kv_in, page_out, page_in,
    load_sem, kv_send, kv_recv, hand_send, back_send, page_send, page_recv,
):
    rows = tokens.shape[0]
    kvh = wkv.shape[0] // ROW
    heads = wq.shape[1] // HD
    group = heads // kvh
    me = lax.axis_index("req")
    my_tp = lax.axis_index("tp")

    odd = lax.rem(me, 2)
    partner = me + 1 - 2 * odd
    evens = range(2, reach + 1, 2)

    kv_width = kvh * HD
    loads = [
        pltpu.make_async_copy(src, dst, load_sem.at[i])
        for i, (src, dst) in enumerate(
            (
                (tokens_hbm, tokens),
                (wk_hbm, wkv.at[:kv_width]),
                (wv_hbm, wkv.at[kv_width:]),
                (wq_hbm, wq),
            )
        )
    ]
    for load in loads:
        load.start()

    barrier = pltpu.get_barrier_semaphore()
    pl.semaphore_signal(barrier, inc=1, device_id={"req": partner}, device_id_type=MESH)
    for d in evens:
        @pl.when(me + d < n_req)
        def _():
            pl.semaphore_signal(barrier, inc=1, device_id={"req": me + d}, device_id_type=MESH)

        @pl.when(me - d >= 0)
        def _():
            pl.semaphore_signal(barrier, inc=1, device_id={"req": me - d}, device_id_type=MESH)
    for o in range(1, n_tp):
        pl.semaphore_signal(
            barrier, inc=1, device_id={"tp": lax.rem(my_tp + o, n_tp)}, device_id_type=MESH
        )

    block_start = me * rows
    slot = block_start + lax.broadcasted_iota(jnp.int32, (1, rows), 1)
    first, last = meta(slot, counts, pads)
    position = (slot - first).astype(F32)
    live = slot <= last
    high = jnp.minimum(slot, last)
    index = lax.broadcasted_iota(jnp.int32, (HD // 2, 1), 0).astype(F32)
    frequency = jnp.exp(index * (-2.0 * math.log(ROPE_BASE) / HD))
    angle = frequency * position
    cosine, sine = jnp.cos(angle), jnp.sin(angle)

    loads[0].wait()
    x = tokens[...].astype(F32)
    scale = lax.rsqrt(jnp.mean(x * x, axis=-1, keepdims=True) + NORM_EPS)
    tokens[...] = (x * scale * gain[...].reshape(1, -1)).astype(BF16)

    loads[1].wait()
    loads[2].wait()
    both = lax.dot_general(
        wkv[...], tokens[...], (((1,), (1,)), ((), ())), preferred_element_type=F32
    )
    key, value = both[:kv_width], both[kv_width:]
    for g in range(kvh):
        at = g * HD
        kv_own[g * ROW : g * ROW + HD] = rotary(key[at : at + HD], cosine, sine).astype(BF16)
        kv_own[g * ROW + HD : (g + 1) * ROW] = value[at : at + HD].astype(BF16)

    ahead = jnp.minimum(reach, n_req - 1 - me) >> 1
    behind = jnp.minimum(reach, me) >> 1
    pl.semaphore_wait(barrier, ahead + behind + n_tp)

    def head(ref, g):
        return ref.at[g * ROW : (g + 1) * ROW]

    def kv_copy(d, g):
        return pltpu.make_async_remote_copy(
            src_ref=head(kv_own, g),
            dst_ref=kv_in.at[d - 1, g * ROW : (g + 1) * ROW],
            send_sem=kv_send.at[d - 1, g],
            recv_sem=kv_recv.at[d - 1, g],
            device_id={"req": me + d},
            device_id_type=MESH,
        )

    def hand_on(e, g):
        to = e - 2 * odd
        return pltpu.make_async_remote_copy(
            src_ref=kv_in.at[e - 1, g * ROW : (g + 1) * ROW] if e else head(kv_own, g),
            dst_ref=kv_in.at[to, g * ROW : (g + 1) * ROW],
            send_sem=hand_send.at[e, g],
            recv_sem=kv_recv.at[to, g],
            device_id={"req": partner},
            device_id_type=MESH,
        )

    def hands_on(e):
        if e == 0:
            return odd == 0
        if e == reach:
            return (odd == 1) & (me - e >= 0)
        return me - e >= 0

    square = n_req == 8 and reach == 4

    def sends(d):
        go = me + d < n_req
        if square and d == 2:
            go = go & ((me < 2) | (me > 3))
        return go

    def pass_back(g):
        return pltpu.make_async_remote_copy(
            src_ref=kv_in.at[3, g * ROW : (g + 1) * ROW],
            dst_ref=kv_in.at[1, g * ROW : (g + 1) * ROW],
            send_sem=back_send.at[g],
            recv_sem=kv_recv.at[1, g],
            device_id={"req": me - 2},
            device_id_type=MESH,
        )

    for g in range(kvh):
        for d in evens:
            @pl.when(sends(d))
            def _():
                kv_copy(d, g).start()

        @pl.when(hands_on(0))
        def _():
            hand_on(0, g).start()

    for d in range(1, reach + 1):
        @pl.when(me - d < 0)
        def _():
            kv_in[d - 1] = jnp.zeros(kv_in.shape[1:], BF16)

    slots_here = rows // PAGE // n_tp
    live_rows = slots_here * kvh
    fold = 16 // live_rows
    pieces = PAGE // fold
    span = pieces * ROW
    bits = [int(math.log2(v)) for v in (kvh, slots_here, fold, n_tp)]
    r = lax.broadcasted_iota(jnp.int32, (pieces * n_tp * 16, 1), 0)
    h_r = r & (kvh - 1)
    r = r >> bits[0]
    slot_r = r & (slots_here - 1)
    r = r >> bits[1]
    fold_r = r & (fold - 1)
    r = r >> bits[2]
    tp_r = r & (n_tp - 1)
    piece_r = r >> bits[3]
    place_r = h_r + kvh * (fold_r * pieces + piece_r + PAGE * (tp_r * slots_here + slot_r))
    in_block = lax.broadcasted_iota(jnp.int32, (1, rows), 1)
    page_at = jnp.zeros_like(in_block)
    for p in range(rows // PAGE):
        page_at = jnp.where((in_block >> 4) == p, table[0, p], page_at)
    place_t = jnp.where(live, kvh * ((in_block & (PAGE - 1)) + PAGE * page_at), -kvh)
    place_c = jnp.concatenate([place_t + h for h in range(kvh)], axis=1)
    pick = jnp.where(place_r == place_c, 1.0, 0.0).astype(BF16)
    kv_wide = jnp.concatenate([kv_own[g * ROW : (g + 1) * ROW] for g in range(kvh)], axis=1)
    placed = lax.dot_general(
        pick, kv_wide, (((1,), (1,)), ((), ())), preferred_element_type=F32
    )
    wide = jnp.concatenate(
        [placed[i * n_tp * 16 : (i + 1) * n_tp * 16] for i in range(pieces)], axis=1
    ).astype(BF16)
    for t in range(n_tp):
        page_out[t] = wide[t * 16 : (t + 1) * 16]

    def page_copy(o):
        to = lax.rem(my_tp + o, n_tp)
        return pltpu.make_async_remote_copy(
            src_ref=page_out.at[to],
            dst_ref=page_in.at[o],
            send_sem=page_send.at[o],
            recv_sem=page_recv.at[o],
            device_id={"tp": to},
            device_id_type=MESH,
        )

    for o in range(1, n_tp):
        page_copy(o).start()
    page_in[0] = page_out[my_tp]

    loads[3].wait()
    query = jnp.dot(tokens[...], wq[...], preferred_element_type=F32).T
    queries = []
    for g in range(kvh):
        parts = []
        for h in range(g * group, (g + 1) * group):
            parts.append(rotary(query[h * HD : (h + 1) * HD], cosine, sine).astype(BF16))
        queries.append(jnp.concatenate(parts, axis=1))

    factor = math.log2(math.e) / math.sqrt(HD)
    ones = jnp.ones((ONES, rows), BF16)
    state = [None] * kvh

    def bias_of(d):
        at = block_start - d * rows + lax.broadcasted_iota(jnp.int32, (rows, 1), 0)
        ok = (at >= first) & (at <= high)
        if (d + 1) * rows > WINDOW:
            ok = ok & (slot - at < WINDOW)
        return jnp.where(ok, 0.0, MASKED)

    def attend(g, blocks, biases):
        scores, values = [], []
        for d, b in zip(blocks, biases):
            src = kv_own if d == 0 else kv_in.at[d - 1]
            s = lax.dot_general(
                src[g * ROW : g * ROW + HD], queries[g], (((0,), (0,)), ((), ())),
                preferred_element_type=F32,
            )
            scores.append(s * factor + jnp.concatenate([b] * group, axis=1))
            values.append(jnp.concatenate([src[g * ROW + HD : (g + 1) * ROW], ones], axis=0))
        top = functools.reduce(
            jnp.maximum, [jnp.max(s, axis=0, keepdims=True) for s in scores]
        )
        if state[g] is not None:
            top = jnp.maximum(top, state[g][0])
        total = None
        for s, v in zip(scores, values):
            w = jnp.exp2(s - top).astype(BF16)
            part = jnp.dot(v, w, preferred_element_type=F32)
            total = part if total is None else total + part
        if state[g] is not None:
            total = total + state[g][1] * jnp.exp2(state[g][0] - top)
        state[g] = (top, total)

    own_bias = [bias_of(0)]
    for g in range(kvh):
        if square:
            @pl.when(me > 5)
            def _():
                kv_copy(4, g).wait_recv()
                pass_back(g).start()
        attend(g, [0], own_bias)
    for g in range(kvh):
        for d in evens:
            due = me - d >= 0
            if square and d == 4:
                due = due & (me < 6)

            @pl.when(due)
            def _():
                kv_copy(d, g).wait_recv()

            @pl.when(hands_on(d))
            def _():
                hand_on(d, g).start()
    biases = [bias_of(d) for d in evens]
    for g in range(kvh):
        attend(g, list(evens), biases)
    odds = range(1, reach + 1, 2)
    biases = [bias_of(d) for d in odds]
    for g in range(kvh):
        for d in odds:
            @pl.when(me - d >= 0)
            def _():
                kv_copy(d, g).wait_recv()
        attend(g, list(odds), biases)
        acc = state[g][1]
        out = acc[:HD] / acc[HD : HD + 1]
        for j in range(group):
            at = (g * group + j) * HD
            context_ref[at : at + HD] = jnp.where(
                live, out[:, j * rows : (j + 1) * rows], 0.0
            ).astype(BF16)

    for o in range(1, n_tp):
        page_copy(o).wait_recv()
    pages_ref[...] = page_in[...]

    for g in range(kvh):
        for d in evens:
            @pl.when(sends(d))
            def _():
                kv_copy(d, g).wait_send()
        for e in range(0, reach + 1, 2):
            @pl.when(hands_on(e))
            def _():
                hand_on(e, g).wait_send()
        if square:
            @pl.when(me > 5)
            def _():
                pass_back(g).wait_send()
    for o in range(1, n_tp):
        page_copy(o).wait_send()


def finish(n_tp, kvh, context_hbm, page_hbm, context_ref, cache_ref, context_t, page_in, load_sem):
    loads = [
        pltpu.make_async_copy(context_hbm, context_t, load_sem.at[0]),
        pltpu.make_async_copy(page_hbm, page_in, load_sem.at[1]),
    ]
    for load in loads:
        load.start()
    loads[0].wait()
    context_ref[...] = context_t[...].T
    slots_here = cache_ref.shape[0]
    fold = 16 // (slots_here * kvh)
    bits = [int(math.log2(v)) for v in (kvh, slots_here)]
    my_tp = lax.axis_index("tp")
    source = lax.broadcasted_iota(jnp.int32, (1, n_tp * 16), 1)
    from_tp = (my_tp - (source >> 4) + n_tp) & (n_tp - 1)
    in_tile = source & 15
    fold_s = in_tile >> (bits[0] + bits[1])
    slot_s = (in_tile >> bits[0]) & (slots_here - 1)
    h_s = in_tile & (kvh - 1)
    goal_s = (slot_s * n_tp + from_tp) * kvh + h_s
    goal = lax.broadcasted_iota(jnp.int32, (slots_here * n_tp * kvh, 1), 0)
    loads[1].wait()
    arrived = page_in[...].reshape(n_tp * 16, page_in.shape[2])
    lanes = []
    for f in range(fold):
        pick_f = jnp.where((goal == goal_s) & (fold_s == f), 1.0, 0.0).astype(BF16)
        lanes.append(jnp.dot(pick_f, arrived, preferred_element_type=F32))
    pages = jnp.concatenate(lanes, axis=1)
    all_heads = n_tp * kvh
    for s in range(slots_here):
        cache_ref[s] = pages[s * all_heads : (s + 1) * all_heads].astype(BF16)


def per_device(tokens, norm_gain, w_query, w_key, w_value, page_counts, pad_counts, page_table):
    rows, width = tokens.shape
    n_req, n_tp = lax.axis_size("req"), lax.axis_size("tp")
    longest = min(8 * rows, rows * n_req // 2)
    reach = min(WINDOW, longest) // rows
    assert reach % 2 == 0 and n_req % 2 == 0
    kv_rows = 2 * w_key.shape[1]
    kvh = w_key.shape[1] // HD
    slots_here = rows // PAGE // n_tp
    span = slots_here * kvh * PAGE * ROW // 16
    vmem = pl.BlockSpec(memory_space=pltpu.VMEM)
    smem = pl.BlockSpec(memory_space=pltpu.SMEM)
    hbm = pl.BlockSpec(memory_space=pltpu.HBM)
    context_t, pages = pl.pallas_call(
        functools.partial(kernel, n_req, n_tp, reach),
        out_shape=(
            jax.ShapeDtypeStruct((w_query.shape[1], rows), BF16),
            jax.ShapeDtypeStruct((n_tp, 16, span), BF16),
        ),
        in_specs=[smem, smem, smem, vmem, hbm, hbm, hbm, hbm],
        out_specs=(vmem, vmem),
        scratch_shapes=[
            pltpu.VMEM((rows, width), BF16),
            pltpu.VMEM((kv_rows, width), BF16),
            pltpu.VMEM(w_query.shape, BF16),
            pltpu.VMEM((kv_rows, rows), BF16),
            pltpu.VMEM((reach, kv_rows, rows), BF16),
            pltpu.VMEM((n_tp, 16, span), BF16),
            pltpu.VMEM((n_tp, 16, span), BF16),
            pltpu.SemaphoreType.DMA((4,)),
            pltpu.SemaphoreType.DMA((reach, kvh)),
            pltpu.SemaphoreType.DMA((reach, kvh)),
            pltpu.SemaphoreType.DMA((reach + 1, kvh)),
            pltpu.SemaphoreType.DMA((kvh,)),
            pltpu.SemaphoreType.DMA((n_tp,)),
            pltpu.SemaphoreType.DMA((n_tp,)),
        ],
        compiler_params=pltpu.CompilerParams(
            collective_id=0, has_side_effects=True, vmem_limit_bytes=56 * 1024 * 1024
        ),
    )(
        page_counts, pad_counts, page_table, norm_gain,
        tokens, w_key.T, w_value.T, w_query,
    )
    return pl.pallas_call(
        functools.partial(finish, n_tp, kvh),
        out_shape=(
            jax.ShapeDtypeStruct((rows, w_query.shape[1]), BF16),
            jax.ShapeDtypeStruct((slots_here, n_tp * kvh, PAGE * ROW), BF16),
        ),
        in_specs=[hbm, hbm],
        out_specs=(vmem, vmem),
        scratch_shapes=[
            pltpu.VMEM((w_query.shape[1], rows), BF16),
            pltpu.VMEM((n_tp, 16, span), BF16),
            pltpu.SemaphoreType.DMA((2,)),
        ],
        compiler_params=pltpu.CompilerParams(vmem_limit_bytes=56 * 1024 * 1024),
    )(context_t, pages)


def solution(mesh):
    in_specs = (
        P("req", None),
        P(),
        P(None, "tp"),
        P(None, "tp"),
        P(None, "tp"),
        P(),
        P(),
        P("req", None),
    )
    out_specs = (P("req", "tp"), P(("req", "tp"), None, None))
    return jax.shard_map(
        per_device, mesh=mesh, in_specs=in_specs, out_specs=out_specs, check_vma=False
    )
```

```python
import functools
import math

import jax
import jax.numpy as jnp
from jax import lax
from jax.experimental import pallas as pl
from jax.experimental.pallas import tpu as pltpu
from jax.sharding import PartitionSpec as P

HD = 80
WINDOW = 4096
PAGE = 16
NORM_EPS = 1e-05
ROPE_BASE = 10000.0
MASKED = -1e30
ROW = 2 * HD
ONES = 16
MESH = pl.DeviceIdType.MESH
F32 = jnp.float32
BF16 = jnp.bfloat16


def meta(slot, counts, pads):
    first = jnp.zeros_like(slot)
    last = jnp.zeros_like(slot)
    start = jnp.int32(0)
    for i in range(counts.shape[0]):
        slots = counts[i] * PAGE
        inside = (slot >= start) & (slot < start + slots)
        first = jnp.where(inside, start, first)
        last = jnp.where(inside, start + slots - pads[i] - 1, last)
        start = start + slots
    return first, last


def rotary(u, cosine, sine):
    half = HD // 2
    u1, u2 = u[:half], u[half:]
    return jnp.concatenate([u1 * cosine - u2 * sine, u2 * cosine + u1 * sine], axis=0)


def kernel(
    n_req, n_tp, reach,
    counts, pads, table, gain, tokens_hbm, wk_hbm, wv_hbm, wq_hbm,
    context_ref, pages_ref,
    tokens, wkv, wq, kv_own, kv_in, page_out, page_in,
    load_sem, kv_send, kv_recv, hand_send, back_send, page_send, page_recv,
):
    rows = tokens.shape[0]
    kvh = wkv.shape[0] // ROW
    heads = wq.shape[1] // HD
    group = heads // kvh
    me = lax.axis_index("req")
    my_tp = lax.axis_index("tp")

    odd = lax.rem(me, 2)
    partner = me + 1 - 2 * odd
    evens = range(2, reach + 1, 2)

    kv_width = kvh * HD
    loads = [
        pltpu.make_async_copy(src, dst, load_sem.at[i])
        for i, (src, dst) in enumerate(
            (
                (tokens_hbm, tokens),
                (wk_hbm, wkv.at[:kv_width]),
                (wv_hbm, wkv.at[kv_width:]),
                (wq_hbm, wq),
            )
        )
    ]
    for load in loads:
        load.start()

    barrier = pltpu.get_barrier_semaphore()
    pl.semaphore_signal(barrier, inc=1, device_id={"req": partner}, device_id_type=MESH)
    for d in evens:
        @pl.when(me + d < n_req)
        def _():
            pl.semaphore_signal(barrier, inc=1, device_id={"req": me + d}, device_id_type=MESH)

        @pl.when(me - d >= 0)
        def _():
            pl.semaphore_signal(barrier, inc=1, device_id={"req": me - d}, device_id_type=MESH)
    for o in range(1, n_tp):
        pl.semaphore_signal(
            barrier, inc=1, device_id={"tp": lax.rem(my_tp + o, n_tp)}, device_id_type=MESH
        )

    block_start = me * rows
    slot = block_start + lax.broadcasted_iota(jnp.int32, (1, rows), 1)
    first, last = meta(slot, counts, pads)
    position = (slot - first).astype(F32)
    live = slot <= last
    high = jnp.minimum(slot, last)
    index = lax.broadcasted_iota(jnp.int32, (HD // 2, 1), 0).astype(F32)
    frequency = jnp.exp(index * (-2.0 * math.log(ROPE_BASE) / HD))
    angle = frequency * position
    cosine, sine = jnp.cos(angle), jnp.sin(angle)

    loads[0].wait()
    x = tokens[...].astype(F32)
    scale = lax.rsqrt(jnp.mean(x * x, axis=-1, keepdims=True) + NORM_EPS)
    tokens[...] = (x * scale * gain[...].reshape(1, -1)).astype(BF16)

    loads[1].wait()
    loads[2].wait()
    both = lax.dot_general(
        wkv[...], tokens[...], (((1,), (1,)), ((), ())), preferred_element_type=F32
    )
    key, value = both[:kv_width], both[kv_width:]
    for g in range(kvh):
        at = g * HD
        kv_own[g * ROW : g * ROW + HD] = rotary(key[at : at + HD], cosine, sine).astype(BF16)
        kv_own[g * ROW + HD : (g + 1) * ROW] = value[at : at + HD].astype(BF16)

    ahead = jnp.minimum(reach, n_req - 1 - me) >> 1
    behind = jnp.minimum(reach, me) >> 1
    pl.semaphore_wait(barrier, ahead + behind + n_tp)

    def head(ref, g):
        return ref.at[g * ROW : (g + 1) * ROW]

    def kv_copy(d, g):
        return pltpu.make_async_remote_copy(
            src_ref=head(kv_own, g),
            dst_ref=kv_in.at[d - 1, g * ROW : (g + 1) * ROW],
            send_sem=kv_send.at[d - 1, g],
            recv_sem=kv_recv.at[d - 1, g],
            device_id={"req": me + d},
            device_id_type=MESH,
        )

    def hand_on(e, g):
        to = e - 2 * odd
        return pltpu.make_async_remote_copy(
            src_ref=kv_in.at[e - 1, g * ROW : (g + 1) * ROW] if e else head(kv_own, g),
            dst_ref=kv_in.at[to, g * ROW : (g + 1) * ROW],
            send_sem=hand_send.at[e, g],
            recv_sem=kv_recv.at[to, g],
            device_id={"req": partner},
            device_id_type=MESH,
        )

    def hands_on(e):
        if e == 0:
            return odd == 0
        if e == reach:
            return (odd == 1) & (me - e >= 0)
        return me - e >= 0

    square = n_req == 8 and reach == 4

    def sends(d, g):
        go = me + d < n_req
        if square and d == 2 and g == 0:
            go = go & ((me < 2) | (me > 3))
        return go

    def pass_back(g):
        return pltpu.make_async_remote_copy(
            src_ref=kv_in.at[3, g * ROW : (g + 1) * ROW],
            dst_ref=kv_in.at[1, g * ROW : (g + 1) * ROW],
            send_sem=back_send.at[g],
            recv_sem=kv_recv.at[1, g],
            device_id={"req": me - 2},
            device_id_type=MESH,
        )

    for g in range(kvh):
        for d in evens:
            @pl.when(sends(d, g))
            def _():
                kv_copy(d, g).start()

        @pl.when(hands_on(0))
        def _():
            hand_on(0, g).start()

    for d in range(1, reach + 1):
        @pl.when(me - d < 0)
        def _():
            kv_in[d - 1] = jnp.zeros(kv_in.shape[1:], BF16)

    slots_here = rows // PAGE // n_tp
    live_rows = slots_here * kvh
    fold = 16 // live_rows
    pieces = PAGE // fold
    span = pieces * ROW
    bits = [int(math.log2(v)) for v in (kvh, slots_here, fold, n_tp)]
    r = lax.broadcasted_iota(jnp.int32, (pieces * n_tp * 16, 1), 0)
    h_r = r & (kvh - 1)
    r = r >> bits[0]
    slot_r = r & (slots_here - 1)
    r = r >> bits[1]
    fold_r = r & (fold - 1)
    r = r >> bits[2]
    tp_r = r & (n_tp - 1)
    piece_r = r >> bits[3]
    place_r = h_r + kvh * (fold_r * pieces + piece_r + PAGE * (tp_r * slots_here + slot_r))
    in_block = lax.broadcasted_iota(jnp.int32, (1, rows), 1)
    page_at = jnp.zeros_like(in_block)
    for p in range(rows // PAGE):
        page_at = jnp.where((in_block >> 4) == p, table[0, p], page_at)
    place_t = jnp.where(live, kvh * ((in_block & (PAGE - 1)) + PAGE * page_at), -kvh)
    place_c = jnp.concatenate([place_t + h for h in range(kvh)], axis=1)
    pick = jnp.where(place_r == place_c, 1.0, 0.0).astype(BF16)
    kv_wide = jnp.concatenate([kv_own[g * ROW : (g + 1) * ROW] for g in range(kvh)], axis=1)
    placed = lax.dot_general(
        pick, kv_wide, (((1,), (1,)), ((), ())), preferred_element_type=F32
    )
    wide = jnp.concatenate(
        [placed[i * n_tp * 16 : (i + 1) * n_tp * 16] for i in range(pieces)], axis=1
    ).astype(BF16)
    for t in range(n_tp):
        page_out[t] = wide[t * 16 : (t + 1) * 16]

    def page_copy(o):
        to = lax.rem(my_tp + o, n_tp)
        return pltpu.make_async_remote_copy(
            src_ref=page_out.at[to],
            dst_ref=page_in.at[o],
            send_sem=page_send.at[o],
            recv_sem=page_recv.at[o],
            device_id={"tp": to},
            device_id_type=MESH,
        )

    for o in range(1, n_tp):
        page_copy(o).start()
    page_in[0] = page_out[my_tp]

    loads[3].wait()
    query = jnp.dot(tokens[...], wq[...], preferred_element_type=F32).T
    queries = []
    for g in range(kvh):
        parts = []
        for h in range(g * group, (g + 1) * group):
            parts.append(rotary(query[h * HD : (h + 1) * HD], cosine, sine).astype(BF16))
        queries.append(jnp.concatenate(parts, axis=1))

    factor = math.log2(math.e) / math.sqrt(HD)
    ones = jnp.ones((ONES, rows), BF16)
    state = [None] * kvh

    def bias_of(d):
        at = block_start - d * rows + lax.broadcasted_iota(jnp.int32, (rows, 1), 0)
        ok = (at >= first) & (at <= high)
        if (d + 1) * rows > WINDOW:
            ok = ok & (slot - at < WINDOW)
        return jnp.where(ok, 0.0, MASKED)

    def attend(g, blocks, biases):
        scores, values = [], []
        for d, b in zip(blocks, biases):
            src = kv_own if d == 0 else kv_in.at[d - 1]
            s = lax.dot_general(
                src[g * ROW : g * ROW + HD], queries[g], (((0,), (0,)), ((), ())),
                preferred_element_type=F32,
            )
            scores.append(s * factor + jnp.concatenate([b] * group, axis=1))
            values.append(jnp.concatenate([src[g * ROW + HD : (g + 1) * ROW], ones], axis=0))
        top = functools.reduce(
            jnp.maximum, [jnp.max(s, axis=0, keepdims=True) for s in scores]
        )
        if state[g] is not None:
            top = jnp.maximum(top, state[g][0])
        total = None
        for s, v in zip(scores, values):
            w = jnp.exp2(s - top).astype(BF16)
            part = jnp.dot(v, w, preferred_element_type=F32)
            total = part if total is None else total + part
        if state[g] is not None:
            total = total + state[g][1] * jnp.exp2(state[g][0] - top)
        state[g] = (top, total)

    own_bias = [bias_of(0)]
    if square:
        @pl.when(me > 5)
        def _():
            kv_copy(4, 0).wait_recv()
            pass_back(0).start()
    for g in range(kvh):
        attend(g, [0], own_bias)
    for d in reversed(evens):
        for g in reversed(range(kvh)):
            due = me - d >= 0
            if square and d == 4 and g == 0:
                due = due & (me < 6)

            @pl.when(due)
            def _():
                kv_copy(d, g).wait_recv()

            @pl.when(hands_on(d))
            def _():
                hand_on(d, g).start()
        biases = [bias_of(d)]
        for g in range(kvh):
            attend(g, [d], biases)
    odds = range(1, reach + 1, 2)
    biases = [bias_of(d) for d in odds]
    for g in range(kvh):
        for d in odds:
            @pl.when(me - d >= 0)
            def _():
                kv_copy(d, g).wait_recv()
        attend(g, list(odds), biases)
        acc = state[g][1]
        out = acc[:HD] / acc[HD : HD + 1]
        for j in range(group):
            at = (g * group + j) * HD
            context_ref[at : at + HD] = jnp.where(
                live, out[:, j * rows : (j + 1) * rows], 0.0
            ).astype(BF16)

    for o in range(1, n_tp):
        page_copy(o).wait_recv()
    pages_ref[...] = page_in[...]

    for g in range(kvh):
        for d in evens:
            @pl.when(sends(d, g))
            def _():
                kv_copy(d, g).wait_send()
        for e in range(0, reach + 1, 2):
            @pl.when(hands_on(e))
            def _():
                hand_on(e, g).wait_send()
    if square:
        @pl.when(me > 5)
        def _():
            pass_back(0).wait_send()
    for o in range(1, n_tp):
        page_copy(o).wait_send()


def finish(n_tp, kvh, context_hbm, page_hbm, context_ref, cache_ref, context_t, page_in, load_sem):
    loads = [
        pltpu.make_async_copy(context_hbm, context_t, load_sem.at[0]),
        pltpu.make_async_copy(page_hbm, page_in, load_sem.at[1]),
    ]
    for load in loads:
        load.start()
    loads[0].wait()
    context_ref[...] = context_t[...].T
    slots_here = cache_ref.shape[0]
    fold = 16 // (slots_here * kvh)
    bits = [int(math.log2(v)) for v in (kvh, slots_here)]
    my_tp = lax.axis_index("tp")
    source = lax.broadcasted_iota(jnp.int32, (1, n_tp * 16), 1)
    from_tp = (my_tp - (source >> 4) + n_tp) & (n_tp - 1)
    in_tile = source & 15
    fold_s = in_tile >> (bits[0] + bits[1])
    slot_s = (in_tile >> bits[0]) & (slots_here - 1)
    h_s = in_tile & (kvh - 1)
    goal_s = (slot_s * n_tp + from_tp) * kvh + h_s
    goal = lax.broadcasted_iota(jnp.int32, (slots_here * n_tp * kvh, 1), 0)
    loads[1].wait()
    arrived = page_in[...].reshape(n_tp * 16, page_in.shape[2])
    lanes = []
    for f in range(fold):
        pick_f = jnp.where((goal == goal_s) & (fold_s == f), 1.0, 0.0).astype(BF16)
        lanes.append(jnp.dot(pick_f, arrived, preferred_element_type=F32))
    pages = jnp.concatenate(lanes, axis=1)
    all_heads = n_tp * kvh
    for s in range(slots_here):
        cache_ref[s] = pages[s * all_heads : (s + 1) * all_heads].astype(BF16)


def per_device(tokens, norm_gain, w_query, w_key, w_value, page_counts, pad_counts, page_table):
    rows, width = tokens.shape
    n_req, n_tp = lax.axis_size("req"), lax.axis_size("tp")
    longest = min(8 * rows, rows * n_req // 2)
    reach = min(WINDOW, longest) // rows
    assert reach % 2 == 0 and n_req % 2 == 0
    kv_rows = 2 * w_key.shape[1]
    kvh = w_key.shape[1] // HD
    slots_here = rows // PAGE // n_tp
    span = slots_here * kvh * PAGE * ROW // 16
    vmem = pl.BlockSpec(memory_space=pltpu.VMEM)
    smem = pl.BlockSpec(memory_space=pltpu.SMEM)
    hbm = pl.BlockSpec(memory_space=pltpu.HBM)
    context_t, pages = pl.pallas_call(
        functools.partial(kernel, n_req, n_tp, reach),
        out_shape=(
            jax.ShapeDtypeStruct((w_query.shape[1], rows), BF16),
            jax.ShapeDtypeStruct((n_tp, 16, span), BF16),
        ),
        in_specs=[smem, smem, smem, vmem, hbm, hbm, hbm, hbm],
        out_specs=(vmem, vmem),
        scratch_shapes=[
            pltpu.VMEM((rows, width), BF16),
            pltpu.VMEM((kv_rows, width), BF16),
            pltpu.VMEM(w_query.shape, BF16),
            pltpu.VMEM((kv_rows, rows), BF16),
            pltpu.VMEM((reach, kv_rows, rows), BF16),
            pltpu.VMEM((n_tp, 16, span), BF16),
            pltpu.VMEM((n_tp, 16, span), BF16),
            pltpu.SemaphoreType.DMA((4,)),
            pltpu.SemaphoreType.DMA((reach, kvh)),
            pltpu.SemaphoreType.DMA((reach, kvh)),
            pltpu.SemaphoreType.DMA((reach + 1, kvh)),
            pltpu.SemaphoreType.DMA((kvh,)),
            pltpu.SemaphoreType.DMA((n_tp,)),
            pltpu.SemaphoreType.DMA((n_tp,)),
        ],
        compiler_params=pltpu.CompilerParams(
            collective_id=0, has_side_effects=True, vmem_limit_bytes=56 * 1024 * 1024
        ),
    )(
        page_counts, pad_counts, page_table, norm_gain,
        tokens, w_key.T, w_value.T, w_query,
    )
    return pl.pallas_call(
        functools.partial(finish, n_tp, kvh),
        out_shape=(
            jax.ShapeDtypeStruct((rows, w_query.shape[1]), BF16),
            jax.ShapeDtypeStruct((slots_here, n_tp * kvh, PAGE * ROW), BF16),
        ),
        in_specs=[hbm, hbm],
        out_specs=(vmem, vmem),
        scratch_shapes=[
            pltpu.VMEM((w_query.shape[1], rows), BF16),
            pltpu.VMEM((n_tp, 16, span), BF16),
            pltpu.SemaphoreType.DMA((2,)),
        ],
        compiler_params=pltpu.CompilerParams(vmem_limit_bytes=56 * 1024 * 1024),
    )(context_t, pages)


def solution(mesh):
    in_specs = (
        P("req", None),
        P(),
        P(None, "tp"),
        P(None, "tp"),
        P(None, "tp"),
        P(),
        P(),
        P("req", None),
    )
    out_specs = (P("req", "tp"), P(("req", "tp"), None, None))
    return jax.shard_map(
        per_device, mesh=mesh, in_specs=in_specs, out_specs=out_specs, check_vma=False
    )
```
